32 devices in a mesh: groups: 2 (over y), tensor: 16 (over z, x, core).
Axes of the slice: x: 2, y: 2, z: 4, core: 2. Of those that a mesh axis runs over, the one named last changes fastest.
Arguments:
- partials: bfloat16 [16, 256, 8192], P('tensor', 'groups'), parts along dimension 1, may hold values from -1000 to 1000
- norm_gain: float32 [8192], replicated, may hold values from 0.1 to 1.9
- head_weight: bfloat16 [8192, 9504], P(None, 'tensor'), may hold values from -30 to 30
- next_ids: int32 [256], P('groups'), parts along dimension 0, may hold values from 0 to 9503
- lengths: int32 [4], P('groups'), parts along dimension 0, may hold values from 16 to 64, as said below
Outputs:
- log_probs: bfloat16 [256, 9504], P(('groups', 'tensor')), parts along dimension 0
- target_logprob: float32 [256], P(('groups', 'tensor')), parts along dimension 0
The draws below stay inside these ranges and needn't reach their ends.
There are 2 independent parts, one for each index of `groups`. The reference program is written for one: setup_inputs(seed, part) draws one part's arguments, and reference() takes and returns one part's arrays. A program takes and returns all parts, laid end to end along the dimension named above; an argument that names none is the same for every part. Nothing has to cross between parts.
Inputs may be any that keep to these rules, and one draw needn't show every extreme that they name: `lengths`: in every draw one micro-batch is full, with 64 valid positions.
All inputs are finite; a program needn't handle non-finite values.
Results may differ from the reference program's by a relative error of at most 0.004.
Values may be sent and summed in bfloat16 or wider, within the bound.
A program may use at most 64 MiB of HBM per device.

```python
import math
import jax
import jax.numpy as jnp
import numpy as np
from jax import lax

D = 8192
MICRO = 2
MB = 64
TOK = 128
VOCAB = 9504
N_TENSOR = 16


def draw_partials(key, part):
    key = jax.random.fold_in(key, 11)
    keys = jax.random.split(key, 4)
    column = jnp.exp(jax.random.uniform(keys[0], (D,), minval=0.0, maxval=math.log(10.0)))
    rowscale = jnp.exp(jax.random.uniform(keys[1], (TOK, 1), minval=0.0, maxval=math.log(10.0)))
    base = jnp.clip(jax.random.normal(keys[2], (N_TENSOR, TOK, D)), -5.0, 5.0)
    owner = jax.random.permutation(keys[3], N_TENSOR)
    block = jnp.arange(TOK) // (TOK // N_TENSOR)
    spiked = jnp.where(block[None, :] == owner[:, None], 6.0, 1.0)
    values = base * spiked[:, :, None] * rowscale[None, :, :] * column[None, None, :] / 4.0
    return values.astype(jnp.bfloat16)


def draw_head_weight(key, part):
    key = jax.random.fold_in(key, 23)
    keys = jax.random.split(key, 2)
    column = jnp.exp(jax.random.uniform(keys[1], (VOCAB,), minval=0.0, maxval=math.log(10.0)))
    base = jnp.clip(jax.random.normal(keys[0], (D, VOCAB)), -5.0, 5.0)
    weight = base * column[None, :] * (0.8 / math.sqrt(D))
    return weight.astype(jnp.bfloat16)


def draw_lengths(key, part):
    key = jax.random.fold_in(key, 37)
    keys = jax.random.split(key, 2)
    counts = jax.random.randint(keys[0], (MICRO,), MB // 4, MB + 1)
    filled = jax.random.randint(keys[1], (), 0, MICRO)
    return jnp.where(jnp.arange(MICRO) == filled, MB, counts).astype(jnp.int32)


def place_ends(result, rng, least, largest):
    place = [jax.random.randint(jax.random.fold_in(rng, axis), (), 0, length) for axis, length in enumerate(result.shape)]
    main_axis = result.shape.index(max(result.shape))
    beside = place[:main_axis] + [(place[main_axis] + 1) % result.shape[main_axis]] + place[main_axis + 1:]
    return result.at[tuple(place)].set(least).at[tuple(beside)].set(largest)


def rank_bounds(amount, skew):
    portions = [(1 << 20) // math.isqrt(standing ** skew) + 1 for standing in range(1, amount + 1)]
    width = 1 + sum(portions) // (1 << 30)
    return np.cumsum(np.array([max(1, weight // width) for weight in portions]))


def ranked_ids(stream_key, dims, count, slope):
    listing = rank_bounds(count, slope)
    ticket = jax.random.randint(jax.random.fold_in(stream_key, 1), dims, 0, int(listing[count - 1]))
    grade = jnp.searchsorted(jnp.asarray(listing, jnp.int32), ticket, side="right")
    return jax.random.permutation(jax.random.fold_in(stream_key, 2), count)[grade].astype(jnp.int32)


def setup_inputs(seed: int = 0, part: int = 0) -> dict:
    key_of = jax.random.split(jax.random.key(seed), 6)
    part_keys = jax.random.split(jax.random.fold_in(key_of[5], part), 6)
    partials = draw_partials(jax.random.fold_in(jax.random.fold_in(key_of[5], part), 71), part)
    norm_gain = jnp.clip(1.0 + 0.18 * jax.random.normal(key_of[1], (D,), jnp.float32), 0.1, 1.9)
    head_weight = draw_head_weight(jax.random.fold_in(key_of[5], 71), part)
    next_ids = place_ends(ranked_ids(part_keys[3], (TOK,), VOCAB, 2), jax.random.fold_in(part_keys[3], 3), 0, VOCAB - 1).astype(jnp.int32)
    lengths = draw_lengths(jax.random.fold_in(jax.random.fold_in(key_of[5], part), 71), part)
    return dict(partials=partials, norm_gain=norm_gain, head_weight=head_weight, next_ids=next_ids, lengths=lengths)


temper = 2.0

def valid_rows(count, lengths):
    position = jnp.arange(count, dtype=jnp.int32)
    batch = position // MB
    offset = position - batch * MB
    micro_ids = jnp.arange(lengths.shape[0], dtype=jnp.int32)
    limit = lax.optimization_barrier(jnp.sum(jnp.where(batch[:, None] == micro_ids[None, :], lengths[None, :], 0), axis=1))
    return offset < limit

def reference(partials, norm_gain, head_weight, next_ids, lengths):
    hidden = lax.optimization_barrier(jnp.sum(partials, axis=0, dtype=jnp.float32))
    scale = lax.rsqrt(lax.optimization_barrier(jnp.mean(hidden * hidden, axis=1, keepdims=True)) + 1e-06)
    normed = (hidden * scale * norm_gain.astype(jnp.float32)).astype(jnp.bfloat16)
    logits = jnp.dot(normed, head_weight, preferred_element_type=jnp.float32) / temper
    top = lax.optimization_barrier(jnp.max(logits, axis=1, keepdims=True))
    logsum = top + jnp.log(lax.optimization_barrier(jnp.sum(jnp.exp(logits - top), axis=1, keepdims=True)))
    logprob = logits - logsum
    valid = valid_rows(logits.shape[0], lengths)
    picked = jnp.take_along_axis(logprob, next_ids[:, None].astype(jnp.int32), axis=1)[:, 0]
    log_probs = jnp.where(valid[:, None], logprob, jnp.float32(0.0)).astype(jnp.bfloat16)
    target_logprob = jnp.where(valid, picked, jnp.float32(0.0))
    return (log_probs, target_logprob)
```

```python
import functools
import jax
import jax.numpy as jnp
from jax import lax
from jax.experimental import pallas as pl
from jax.experimental.pallas import tpu as pltpu
from jax.sharding import PartitionSpec as P

MB = 64


temper = 2.0


def valid_rows(count, lengths):
    position = jnp.arange(count, dtype=jnp.int32)
    batch = position // MB
    offset = position - batch * MB
    micro_ids = jnp.arange(lengths.shape[0], dtype=jnp.int32)
    limit = jnp.sum(jnp.where(batch[:, None] == micro_ids[None, :], lengths[None, :], 0), axis=1)
    return offset < limit


def rms_normed(hidden, norm_gain):
    scale = lax.rsqrt(jnp.mean(hidden * hidden, axis=1, keepdims=True) + 1e-06)
    return (hidden * scale * norm_gain).astype(jnp.bfloat16)


def on_device_plain(partials, norm_gain, head_weight, next_ids, lengths):
    rows_all = partials.shape[1]
    own_rows = rows_all // lax.axis_size("tensor")
    first_row = lax.axis_index("tensor") * own_rows
    term = jnp.sum(partials, axis=0, dtype=jnp.float32)
    hidden = lax.psum(term, "tensor")
    normed = rms_normed(hidden, norm_gain)
    logits = jnp.dot(normed, head_weight, preferred_element_type=jnp.float32) / temper
    valid_all = valid_rows(rows_all, lengths)
    regrouped = lax.all_to_all(logits, "tensor", split_axis=0, concat_axis=1, tiled=True)
    top = jnp.max(regrouped, axis=1, keepdims=True)
    logsum = top + jnp.log(jnp.sum(jnp.exp(regrouped - top), axis=1, keepdims=True))
    logprob = regrouped - logsum
    ids_own = lax.dynamic_slice_in_dim(next_ids, first_row, own_rows)
    valid_own = lax.dynamic_slice_in_dim(valid_all, first_row, own_rows)
    columns = jnp.arange(regrouped.shape[1], dtype=jnp.int32)
    picked = jnp.sum(jnp.where(columns[None, :] == ids_own[:, None], logprob, 0.0), axis=1)
    log_probs = jnp.where(valid_own[:, None], logprob, 0.0).astype(jnp.bfloat16)
    target_logprob = jnp.where(valid_own, picked, 0.0)
    return (log_probs, target_logprob)


HALVES = 2


def head_kernel(n, X, Z, part_ref, gain_ref, w_ref, ids_ref, len_ref, out_ref, tgt_ref,
                pv, wv, rc, xs, xr, zs, zr, hb, acc, oacc, ssq, dbuf, frecv, sbuf, srecv,
                loc_sem, c_ss, c_rs, x_ss, x_rs, z_ss, z_rs, gz_ss, gz_rs, gx_ss, gx_rs, gc_ss, gc_rs,
                f_ss, f_rs, s_ss, s_rs):
    f32 = jnp.float32
    me = lax.axis_index("tensor")
    c = lax.rem(me, 2)
    x = lax.rem(lax.div(me, 2), X)
    z = lax.div(me, 2 * X)
    T, half = pv.shape
    F = half // (X * Z)
    TH = T // HALVES
    N, D = wv.shape
    own = out_ref.shape[0]

    def dev(zz, xx, cc):
        return {"tensor": (zz * X + xx) * 2 + cc}

    def place(cc, xx, zz):
        return (cc * X + xx) * Z + zz

    def up(v, k, m):
        return lax.rem(v + k, m)

    def down(v, k, m):
        return lax.rem(v + m - k, m)

    def remote(src, dst, ss, rs, to):
        return pltpu.make_async_remote_copy(src_ref=src, dst_ref=dst, send_sem=ss, recv_sem=rs, device_id=to,
                                            device_id_type=pl.DeviceIdType.MESH)

    core_dev = dev(z, x, 1 - c)
    w_copy = pltpu.make_async_copy(w_ref, wv, loc_sem.at[0])
    p_copy = pltpu.make_async_copy(part_ref.at[0, :, pl.ds(pl.multiple_of(c * half, half), half)], pv, loc_sem.at[1])
    p_copy.start()
    w_copy.start()

    barrier = pltpu.get_barrier_semaphore()
    for j in range(1, n):
        pl.semaphore_signal(barrier, inc=1, device_id={"tensor": up(me, j, n)}, device_id_type=pl.DeviceIdType.MESH)
    pl.semaphore_wait(barrier, n - 1)

    sent = []

    def go(copy):
        copy.start()
        sent.append(copy)

    def rows(h):
        return pl.ds(h * TH, TH)

    wide = Z * F
    for h in range(HALVES):
        for j in range(X):
            xx = up(x, 1 + j, X)
            src = part_ref.at[0, rows(h), pl.ds(pl.multiple_of((1 - c) * half + xx * wide, wide), wide)]
            dst = rc.at[rows(h), pl.ds(pl.multiple_of(xx * wide, wide), wide)]
            go(remote(src, dst, c_ss.at[h, j], c_rs.at[h, j], core_dev))
    p_copy.wait()

    def core_wait(h, j):
        dst = rc.at[rows(h), pl.ds(pl.multiple_of(up(x, 1 + j, X) * wide, wide), wide)]
        remote(dst, dst, c_ss.at[h, j], c_rs.at[h, j], core_dev).wait_recv()

    order = sorted(range(1, Z), key=lambda k: abs(k - Z // 2)) + [0]

    def pair_sum(h, xx, zz):
        cols = pl.ds(pl.multiple_of((xx * Z + zz) * F, F), F)
        return pv[rows(h), cols].astype(f32) + rc[rows(h), cols].astype(f32)

    def reduce_x(h):
        for j in range(X - 1):
            xx = up(x, 1 + j, X)
            core_wait(h, j)
            for k in order:
                zz = up(z, k, Z)
                xs[xx, zz, rows(h)] = pair_sum(h, xx, zz).astype(jnp.bfloat16)
                go(remote(xs.at[xx, zz, rows(h)], xr.at[x, zz, rows(h)], x_ss.at[h, j, k], x_rs.at[h, j, k], dev(z, xx, c)))

    def reduce_z(h, ks):
        if ks[0] == order[0]:
            core_wait(h, X - 1)
        for k in ks:
            zz = up(z, k, Z)
            total = pair_sum(h, x, zz)
            for j in range(X - 1):
                xx = down(x, 1 + j, X)
                got = xr.at[xx, zz, rows(h)]
                remote(got, got, x_ss.at[h, j, k], x_rs.at[h, j, k], core_dev).wait_recv()
                total = total + xr[xx, zz, rows(h)].astype(f32)
            if k == 0:
                oacc[rows(h)] = total
            else:
                zs[zz, rows(h)] = total.astype(jnp.bfloat16)
                go(remote(zs.at[zz, rows(h)], zr.at[z, rows(h)], z_ss.at[h, k], z_rs.at[h, k], dev(zz, x, c)))

    def spread(h, p, xo, k):
        piece = hb.at[p, rows(h)]
        go(remote(piece, piece, gc_ss.at[h, xo, k], gc_rs.at[h, xo, k], core_dev))

    def spread_x(h, p, k):
        piece = hb.at[p, rows(h)]
        for j in range(X - 1):
            go(remote(piece, piece, gx_ss.at[h, j, k], gx_rs.at[h, j, k], dev(z, up(x, 1 + j, X), c)))

    def reduce_end(h):
        total = oacc[rows(h)]
        for k in order[:-1]:
            zz = down(z, k, Z)
            got = zr.at[zz, rows(h)]
            remote(got, got, z_ss.at[h, k], z_rs.at[h, k], core_dev).wait_recv()
            total = total + zr[zz, rows(h)].astype(f32)
        p = place(c, x, z)
        hb[p, rows(h)] = (total * gain_ref[:, pl.ds(pl.multiple_of(p * F, F), F)]).astype(jnp.bfloat16)
        piece = hb.at[p, rows(h)]
        for k in order[:-1]:
            go(remote(piece, piece, gz_ss.at[h, k], gz_rs.at[h, k], dev(up(z, k, Z), x, c)))
        spread_x(h, p, 0)
        spread(h, p, 0, 0)

    def gather_z(h):
        for k in order[:-1]:
            p = place(c, x, down(z, k, Z))
            piece = hb.at[p, rows(h)]
            remote(piece, piece, gz_ss.at[h, k], gz_rs.at[h, k], core_dev).wait_recv()
            spread_x(h, p, k)
            spread(h, p, 0, k)

    def gather_x(h):
        for k in [0] + order[:-1]:
            for j in range(X - 1):
                p = place(c, down(x, 1 + j, X), down(z, k, Z))
                piece = hb.at[p, rows(h)]
                remote(piece, piece, gx_ss.at[h, j, k], gx_rs.at[h, j, k], core_dev).wait_recv()
                spread(h, p, 1 + j, k)

    def multiply(h, from_core):
        cc = 1 - c if from_core else c

        def body(i, carry):
            xo = lax.div(i, Z)
            k = lax.rem(i, Z)
            p = place(cc, down(x, xo, X), down(z, k, Z))
            if from_core:
                piece = hb.at[p, rows(h)]
                remote(piece, piece, gc_ss.at[h, xo, k], gc_rs.at[h, xo, k], core_dev).wait_recv()
            start = pl.multiple_of(p * F, F)
            block = hb[p, rows(h)]
            acc[rows(h)] += lax.dot_general(block, wv[:, pl.ds(start, F)], (((1,), (1,)), ((), ())),
                                             preferred_element_type=f32)
            plain = block.astype(f32) * (1.0 / gain_ref[:, pl.ds(start, F)])
            square = plain * plain
            part = square[:, :128]
            for s in range(128, F, 128):
                part = part + square[:, s:s + 128]
            ssq[rows(h)] += part
            return carry

        lax.fori_loop(0, X * Z, body, 0)

    def final_copies(s):
        return (remote(dbuf.at[s], frecv.at[me], f_ss.at[s], f_rs.at[me], {"tensor": jnp.int32(s)}),
                remote(sbuf.at[s], srecv.at[me], s_ss.at[s], s_rs.at[me], {"tensor": jnp.int32(s)}))

    def finish(h):
        scale = lax.rsqrt(jnp.sum(ssq[rows(h)], axis=1, keepdims=True) * (1.0 / D) + 1e-06) * (1.0 / temper)
        logits = acc[rows(h)] * scale
        top = jnp.max(logits, axis=1, keepdims=True)
        low = logits - top
        total = jnp.sum(jnp.exp(low), axis=1, keepdims=True)
        ids = ids_ref[:, :].astype(f32)
        r = lax.broadcasted_iota(jnp.int32, (TH, T), 0) + h * TH
        t = lax.broadcasted_iota(jnp.int32, (TH, T), 1)
        ids = jnp.sum(jnp.where(r == t, ids, 0.0), axis=1, keepdims=True).astype(jnp.int32)
        column = lax.broadcasted_iota(jnp.int32, (TH, N), 1) + me * N
        pick = jnp.sum(jnp.where(column == ids, logits, 0.0), axis=1, keepdims=True)
        lane = lax.broadcasted_iota(jnp.int32, (TH, 128), 1)
        stat = jnp.where(lane == 0, top, jnp.where(lane == 1, total, pick))
        for i in range(TH // own):
            s = h * (TH // own) + i
            mine = low[i * own:(i + 1) * own].astype(jnp.bfloat16)
            facts = stat[i * own:(i + 1) * own]
            dbuf[s] = mine
            sbuf[s] = facts

            @pl.when(me != s)
            def _():
                for copy in final_copies(s):
                    copy.start()

            @pl.when(me == s)
            def _():
                frecv[s] = mine
                srecv[s] = facts

    acc[...] = jnp.zeros_like(acc)
    ssq[...] = jnp.zeros_like(ssq)
    reduce_x(0)
    reduce_x(1)
    reduce_z(0, order)
    reduce_z(1, order[:1])
    reduce_end(0)
    reduce_z(1, order[1:])
    gather_z(0)
    reduce_end(1)
    gather_x(0)
    w_copy.wait()
    multiply(0, False)
    gather_z(1)
    multiply(0, True)
    finish(0)
    gather_x(1)
    multiply(1, False)
    multiply(1, True)
    finish(1)

    for s in range(n):
        @pl.when(me != s)
        def _():
            remote(frecv.at[s], frecv.at[s], f_ss.at[s], f_rs.at[s], core_dev).wait_recv()
            remote(srecv.at[s], srecv.at[s], s_ss.at[s], s_rs.at[s], core_dev).wait_recv()

    tops = [srecv[s][:, 0:1] for s in range(n)]
    top = functools.reduce(jnp.maximum, tops)
    total = sum(srecv[s][:, 1:2] * jnp.exp(tops[s] - top) for s in range(n))
    pick = sum(srecv[s][:, 2:3] for s in range(n))
    logsum = top + jnp.log(total)
    position = lax.broadcasted_iota(jnp.int32, (own, 1), 0) + me * own
    batch = lax.div(position, MB)
    limit = jnp.zeros((own, 1), jnp.int32)
    for m in range(T // MB):
        limit = jnp.where(batch == m, len_ref[m], limit)
    valid = position - batch * MB < limit
    for s in range(n):
        value = frecv[s].astype(f32) + (tops[s] - logsum)
        out_ref[:, s * N:(s + 1) * N] = jnp.where(valid, value, 0.0).astype(jnp.bfloat16)
    target = jnp.where(valid, pick - logsum, 0.0)
    r = lax.broadcasted_iota(jnp.int32, (own, own), 0)
    t = lax.broadcasted_iota(jnp.int32, (own, own), 1)
    tgt_ref[...] = jnp.sum(jnp.where(r == t, target, 0.0), axis=0, keepdims=True)

    for copy in sent:
        copy.wait_send()
    for s in range(n):
        @pl.when(me != s)
        def _():
            for copy in final_copies(s):
                copy.wait_send()


def on_device(partials, norm_gain, head_weight, next_ids, lengths):
    n = lax.axis_size("tensor")
    terms, T, D = partials.shape
    N = head_weight.shape[1]
    own = T // n
    F = D // n
    if terms != 1 or F % 128 or own % 8 or n & (n - 1) or T % (MB * HALVES):
        return on_device_plain(partials, norm_gain, head_weight, next_ids, lengths)
    X = 1 << (((n // 2).bit_length() - 1) // 3)
    Z = n // 2 // X
    H = HALVES
    bf16, f32 = jnp.bfloat16, jnp.float32
    dma = pltpu.SemaphoreType.DMA
    vmem = pl.BlockSpec(memory_space=pltpu.VMEM)
    hbm = pl.BlockSpec(memory_space=pl.ANY)
    sems = [(2,)] + [(H, X)] * 2 + [(H, X, Z)] * 2 + [(H, Z)] * 4 + [(H, X, Z)] * 4 + [(n,)] * 4
    out, target = pl.pallas_call(
        functools.partial(head_kernel, n, X, Z),
        out_shape=(jax.ShapeDtypeStruct((own, n * N), bf16), jax.ShapeDtypeStruct((1, own), f32)),
        in_specs=[hbm, vmem, hbm, vmem, pl.BlockSpec(memory_space=pltpu.SMEM)],
        out_specs=(vmem, vmem),
        scratch_shapes=[
            pltpu.VMEM((T, D // 2), bf16), pltpu.VMEM((N, D), bf16), pltpu.VMEM((T, D // 2), bf16),
            pltpu.VMEM((X, Z, T, F), bf16), pltpu.VMEM((X, Z, T, F), bf16),
            pltpu.VMEM((Z, T, F), bf16), pltpu.VMEM((Z, T, F), bf16), pltpu.VMEM((n, T, F), bf16),
            pltpu.VMEM((T, N), f32), pltpu.VMEM((T, F), f32), pltpu.VMEM((T, 128), f32),
            pltpu.VMEM((n, own, N), bf16), pltpu.VMEM((n, own, N), bf16),
            pltpu.VMEM((n, own, 128), f32), pltpu.VMEM((n, own, 128), f32),
        ] + [dma(shape) for shape in sems],
        compiler_params=pltpu.CompilerParams(collective_id=0, has_side_effects=True, vmem_limit_bytes=48 << 20),
        cost_estimate=pl.CostEstimate(flops=2 * T * D * N, bytes_accessed=2 * D * (T + N), transcendentals=T * N),
    )(partials, norm_gain[None, :], head_weight.T, next_ids[None, :], lengths)
    return out, target.reshape(own)


def solution(mesh):
    return jax.shard_map(
        on_device,
        mesh=mesh,
        in_specs=(P("tensor", "groups", None), P(), P(None, "tensor"), P("groups"), P("groups")),
        out_specs=(P(("groups", "tensor"), None), P(("groups", "tensor"))),
        check_vma=False,
    )
```

```python
import functools
import jax
import jax.numpy as jnp
from jax import lax
from jax.experimental import pallas as pl
from jax.experimental.pallas import tpu as pltpu
from jax.sharding import PartitionSpec as P

MB = 64


temper = 2.0


def valid_rows(count, lengths):
    position = jnp.arange(count, dtype=jnp.int32)
    batch = position // MB
    offset = position - batch * MB
    micro_ids = jnp.arange(lengths.shape[0], dtype=jnp.int32)
    limit = jnp.sum(jnp.where(batch[:, None] == micro_ids[None, :], lengths[None, :], 0), axis=1)
    return offset < limit


def rms_normed(hidden, norm_gain):
    scale = lax.rsqrt(jnp.mean(hidden * hidden, axis=1, keepdims=True) + 1e-06)
    return (hidden * scale * norm_gain).astype(jnp.bfloat16)


def on_device_plain(partials, norm_gain, head_weight, next_ids, lengths):
    rows_all = partials.shape[1]
    own_rows = rows_all // lax.axis_size("tensor")
    first_row = lax.axis_index("tensor") * own_rows
    term = jnp.sum(partials, axis=0, dtype=jnp.float32)
    hidden = lax.psum(term, "tensor")
    normed = rms_normed(hidden, norm_gain)
    logits = jnp.dot(normed, head_weight, preferred_element_type=jnp.float32) / temper
    valid_all = valid_rows(rows_all, lengths)
    regrouped = lax.all_to_all(logits, "tensor", split_axis=0, concat_axis=1, tiled=True)
    top = jnp.max(regrouped, axis=1, keepdims=True)
    logsum = top + jnp.log(jnp.sum(jnp.exp(regrouped - top), axis=1, keepdims=True))
    logprob = regrouped - logsum
    ids_own = lax.dynamic_slice_in_dim(next_ids, first_row, own_rows)
    valid_own = lax.dynamic_slice_in_dim(valid_all, first_row, own_rows)
    columns = jnp.arange(regrouped.shape[1], dtype=jnp.int32)
    picked = jnp.sum(jnp.where(columns[None, :] == ids_own[:, None], logprob, 0.0), axis=1)
    log_probs = jnp.where(valid_own[:, None], logprob, 0.0).astype(jnp.bfloat16)
    target_logprob = jnp.where(valid_own, picked, 0.0)
    return (log_probs, target_logprob)


HALVES = 2
CHUNKS = 4
LAGS = (0, 1, 2, 3)


def head_kernel(n, X, Z, part_ref, gain_ref, w_ref, ids_ref, len_ref, out_ref, tgt_ref,
                pv, wv, rc, xs, xr, zs, zr, hb, acc, oacc, ssq, dbuf, frecv, sbuf, srecv,
                loc_sem, c_ss, c_rs, x_ss, x_rs, z_ss, z_rs, gz_ss, gz_rs, gx_ss, gx_rs, gc_ss, gc_rs,
                f_ss, f_rs, s_ss, s_rs):
    f32 = jnp.float32
    me = lax.axis_index("tensor")
    c = lax.rem(me, 2)
    x = lax.rem(lax.div(me, 2), X)
    z = lax.div(me, 2 * X)
    T, half = pv.shape
    F = half // (X * Z)
    TH = T // HALVES
    TC = T // CHUNKS
    per = CHUNKS // HALVES
    N, D = wv.shape
    own = out_ref.shape[0]

    def dev(zz, xx, cc):
        return {"tensor": (zz * X + xx) * 2 + cc}

    def place(cc, xx, zz):
        return (cc * X + xx) * Z + zz

    def up(v, k, m):
        return lax.rem(v + k, m)

    def down(v, k, m):
        return lax.rem(v + m - k, m)

    def remote(src, dst, ss, rs, to):
        return pltpu.make_async_remote_copy(src_ref=src, dst_ref=dst, send_sem=ss, recv_sem=rs, device_id=to,
                                            device_id_type=pl.DeviceIdType.MESH)

    core_dev = dev(z, x, 1 - c)
    w_copy = pltpu.make_async_copy(w_ref, wv, loc_sem.at[0])
    p_copy = pltpu.make_async_copy(part_ref.at[0, :, pl.ds(pl.multiple_of(c * half, half), half)], pv, loc_sem.at[1])
    p_copy.start()
    w_copy.start()

    barrier = pltpu.get_barrier_semaphore()
    for j in range(1, n):
        pl.semaphore_signal(barrier, inc=1, device_id={"tensor": up(me, j, n)}, device_id_type=pl.DeviceIdType.MESH)
    pl.semaphore_wait(barrier, n - 1)

    sent = []

    def go(copy):
        copy.start()
        sent.append(copy)

    def rows(h):
        return pl.ds(h * TC, TC)

    def half_rows(g):
        return pl.ds(g * TH, TH)

    wide = Z * F
    for j, h in [(j, h) for j in range(X - 1) for h in range(CHUNKS)] + [(X - 1, h) for h in range(CHUNKS)]:
            xx = up(x, 1 + j, X)
            src = part_ref.at[0, rows(h), pl.ds(pl.multiple_of((1 - c) * half + xx * wide, wide), wide)]
            dst = rc.at[rows(h), pl.ds(pl.multiple_of(xx * wide, wide), wide)]
            go(remote(src, dst, c_ss.at[h, j], c_rs.at[h, j], core_dev))
    p_copy.wait()

    def core_wait(h, j):
        dst = rc.at[rows(h), pl.ds(pl.multiple_of(up(x, 1 + j, X) * wide, wide), wide)]
        remote(dst, dst, c_ss.at[h, j], c_rs.at[h, j], core_dev).wait_recv()

    order = sorted(range(1, Z), key=lambda k: abs(k - Z // 2)) + [0]

    def pair_sum(h, xx, zz):
        cols = pl.ds(pl.multiple_of((xx * Z + zz) * F, F), F)
        return pv[rows(h), cols].astype(f32) + rc[rows(h), cols].astype(f32)

    def reduce_x(h):
        for j in range(X - 1):
            xx = up(x, 1 + j, X)
            core_wait(h, j)
            for k in order:
                zz = up(z, k, Z)
                xs[xx, zz, rows(h)] = pair_sum(h, xx, zz).astype(jnp.bfloat16)
                go(remote(xs.at[xx, zz, rows(h)], xr.at[x, zz, rows(h)], x_ss.at[h, j, k], x_rs.at[h, j, k], dev(z, xx, c)))

    def reduce_z(h, ks):
        if ks[0] == order[0]:
            core_wait(h, X - 1)
        for k in ks:
            zz = up(z, k, Z)
            total = pair_sum(h, x, zz)
            for j in range(X - 1):
                xx = down(x, 1 + j, X)
                got = xr.at[xx, zz, rows(h)]
                remote(got, got, x_ss.at[h, j, k], x_rs.at[h, j, k], core_dev).wait_recv()
                total = total + xr[xx, zz, rows(h)].astype(f32)
            if k == 0:
                oacc[rows(h)] = total
            else:
                zs[zz, rows(h)] = total.astype(jnp.bfloat16)
                go(remote(zs.at[zz, rows(h)], zr.at[z, rows(h)], z_ss.at[h, k], z_rs.at[h, k], dev(zz, x, c)))

    def spread(h, p, xo, k):
        piece = hb.at[p, rows(h)]
        go(remote(piece, piece, gc_ss.at[h, xo, k], gc_rs.at[h, xo, k], core_dev))

    def spread_x(h, p, k):
        piece = hb.at[p, rows(h)]
        for j in range(X - 1):
            go(remote(piece, piece, gx_ss.at[h, j, k], gx_rs.at[h, j, k], dev(z, up(x, 1 + j, X), c)))

    def reduce_end(h):
        total = oacc[rows(h)]
        for k in order[:-1]:
            zz = down(z, k, Z)
            got = zr.at[zz, rows(h)]
            remote(got, got, z_ss.at[h, k], z_rs.at[h, k], core_dev).wait_recv()
            total = total + zr[zz, rows(h)].astype(f32)
        p = place(c, x, z)
        hb[p, rows(h)] = (total * gain_ref[:, pl.ds(pl.multiple_of(p * F, F), F)]).astype(jnp.bfloat16)
        piece = hb.at[p, rows(h)]
        for k in order[:-1]:
            go(remote(piece, piece, gz_ss.at[h, k], gz_rs.at[h, k], dev(up(z, k, Z), x, c)))
        spread_x(h, p, 0)
        spread(h, p, 0, 0)

    def gather_z(h):
        for k in order[:-1]:
            p = place(c, x, down(z, k, Z))
            piece = hb.at[p, rows(h)]
            remote(piece, piece, gz_ss.at[h, k], gz_rs.at[h, k], core_dev).wait_recv()
            spread_x(h, p, k)
            spread(h, p, 0, k)

    def gather_x(h):
        for k in [0] + order[:-1]:
            for j in range(X - 1):
                p = place(c, down(x, 1 + j, X), down(z, k, Z))
                piece = hb.at[p, rows(h)]
                remote(piece, piece, gx_ss.at[h, j, k], gx_rs.at[h, j, k], core_dev).wait_recv()
                spread(h, p, 1 + j, k)

    def multiply(g, from_core):
        cc = 1 - c if from_core else c

        def body(i, carry):
            xo = lax.div(i, Z)
            k = lax.rem(i, Z)
            p = place(cc, down(x, xo, X), down(z, k, Z))
            if from_core:
                for h in range(g * per, (g + 1) * per):
                    piece = hb.at[p, rows(h)]
                    remote(piece, piece, gc_ss.at[h, xo, k], gc_rs.at[h, xo, k], core_dev).wait_recv()
            start = pl.multiple_of(p * F, F)
            block = hb[p, half_rows(g)]
            acc[half_rows(g)] += lax.dot_general(block, wv[:, pl.ds(start, F)], (((1,), (1,)), ((), ())),
                                             preferred_element_type=f32)
            plain = block.astype(f32) * (1.0 / gain_ref[:, pl.ds(start, F)])
            square = plain * plain
            part = square[:, :128]
            for s in range(128, F, 128):
                part = part + square[:, s:s + 128]
            ssq[half_rows(g)] += part
            return carry

        lax.fori_loop(0, X * Z, body, 0)

    def final_copies(s):
        return (remote(dbuf.at[s], frecv.at[me], f_ss.at[s], f_rs.at[me], {"tensor": jnp.int32(s)}),
                remote(sbuf.at[s], srecv.at[me], s_ss.at[s], s_rs.at[me], {"tensor": jnp.int32(s)}))

    def finish(h):
        scale = lax.rsqrt(jnp.sum(ssq[half_rows(h)], axis=1, keepdims=True) * (1.0 / D) + 1e-06) * (1.0 / temper)
        logits = acc[half_rows(h)] * scale
        top = jnp.max(logits, axis=1, keepdims=True)
        low = logits - top
        total = jnp.sum(jnp.exp(low), axis=1, keepdims=True)
        ids = ids_ref[:, :].astype(f32)
        r = lax.broadcasted_iota(jnp.int32, (TH, T), 0) + h * TH
        t = lax.broadcasted_iota(jnp.int32, (TH, T), 1)
        ids = jnp.sum(jnp.where(r == t, ids, 0.0), axis=1, keepdims=True).astype(jnp.int32)
        column = lax.broadcasted_iota(jnp.int32, (TH, N), 1) + me * N
        pick = jnp.sum(jnp.where(column == ids, logits, 0.0), axis=1, keepdims=True)
        lane = lax.broadcasted_iota(jnp.int32, (TH, 128), 1)
        stat = jnp.where(lane == 0, top, jnp.where(lane == 1, total, pick))
        for i in range(TH // own):
            s = h * (TH // own) + i
            mine = low[i * own:(i + 1) * own].astype(jnp.bfloat16)
            facts = stat[i * own:(i + 1) * own]
            dbuf[s] = mine
            sbuf[s] = facts

            @pl.when(me != s)
            def _():
                for copy in final_copies(s):
                    copy.start()

            @pl.when(me == s)
            def _():
                frecv[s] = mine
                srecv[s] = facts

    acc[...] = jnp.zeros_like(acc)
    ssq[...] = jnp.zeros_like(ssq)
    for h in range(CHUNKS):
        reduce_x(h)
    stages = (lambda h: reduce_z(h, order), reduce_end, gather_z, gather_x)
    for step in range(CHUNKS + LAGS[-1]):
        for stage, lag in zip(stages, LAGS):
            if 0 <= step - lag < CHUNKS:
                stage(step - lag)
        done = step - LAGS[-1] + 1
        if done == per:
            w_copy.wait()
            multiply(0, False)
        if done == per + 1:
            multiply(0, True)
            finish(0)
    for g in range(1, HALVES):
        multiply(g, False)
        multiply(g, True)
        finish(g)

    for s in range(n):
        @pl.when(me != s)
        def _():
            remote(frecv.at[s], frecv.at[s], f_ss.at[s], f_rs.at[s], core_dev).wait_recv()
            remote(srecv.at[s], srecv.at[s], s_ss.at[s], s_rs.at[s], core_dev).wait_recv()

    tops = [srecv[s][:, 0:1] for s in range(n)]
    top = functools.reduce(jnp.maximum, tops)
    total = sum(srecv[s][:, 1:2] * jnp.exp(tops[s] - top) for s in range(n))
    pick = sum(srecv[s][:, 2:3] for s in range(n))
    logsum = top + jnp.log(total)
    position = lax.broadcasted_iota(jnp.int32, (own, 1), 0) + me * own
    batch = lax.div(position, MB)
    limit = jnp.zeros((own, 1), jnp.int32)
    for m in range(T // MB):
        limit = jnp.where(batch == m, len_ref[m], limit)
    valid = position - batch * MB < limit
    for s in range(n):
        value = frecv[s].astype(f32) + (tops[s] - logsum)
        out_ref[:, s * N:(s + 1) * N] = jnp.where(valid, value, 0.0).astype(jnp.bfloat16)
    target = jnp.where(valid, pick - logsum, 0.0)
    r = lax.broadcasted_iota(jnp.int32, (own, own), 0)
    t = lax.broadcasted_iota(jnp.int32, (own, own), 1)
    tgt_ref[...] = jnp.sum(jnp.where(r == t, target, 0.0), axis=0, keepdims=True)

    for copy in sent:
        copy.wait_send()
    for s in range(n):
        @pl.when(me != s)
        def _():
            for copy in final_copies(s):
                copy.wait_send()


def on_device(partials, norm_gain, head_weight, next_ids, lengths):
    n = lax.axis_size("tensor")
    terms, T, D = partials.shape
    N = head_weight.shape[1]
    own = T // n
    F = D // n
    if terms != 1 or F % 128 or own % 8 or n & (n - 1) or T % (16 * CHUNKS):
        return on_device_plain(partials, norm_gain, head_weight, next_ids, lengths)
    X = 1 << (((n // 2).bit_length() - 1) // 3)
    Z = n // 2 // X
    H = CHUNKS
    bf16, f32 = jnp.bfloat16, jnp.float32
    dma = pltpu.SemaphoreType.DMA
    vmem = pl.BlockSpec(memory_space=pltpu.VMEM)
    hbm = pl.BlockSpec(memory_space=pl.ANY)
    sems = [(2,)] + [(H, X)] * 2 + [(H, X, Z)] * 2 + [(H, Z)] * 4 + [(H, X, Z)] * 4 + [(n,)] * 4
    out, target = pl.pallas_call(
        functools.partial(head_kernel, n, X, Z),
        out_shape=(jax.ShapeDtypeStruct((own, n * N), bf16), jax.ShapeDtypeStruct((1, own), f32)),
        in_specs=[hbm, vmem, hbm, vmem, pl.BlockSpec(memory_space=pltpu.SMEM)],
        out_specs=(vmem, vmem),
        scratch_shapes=[
            pltpu.VMEM((T, D // 2), bf16), pltpu.VMEM((N, D), bf16), pltpu.VMEM((T, D // 2), bf16),
            pltpu.VMEM((X, Z, T, F), bf16), pltpu.VMEM((X, Z, T, F), bf16),
            pltpu.VMEM((Z, T, F), bf16), pltpu.VMEM((Z, T, F), bf16), pltpu.VMEM((n, T, F), bf16),
            pltpu.VMEM((T, N), f32), pltpu.VMEM((T, F), f32), pltpu.VMEM((T, 128), f32),
            pltpu.VMEM((n, own, N), bf16), pltpu.VMEM((n, own, N), bf16),
            pltpu.VMEM((n, own, 128), f32), pltpu.VMEM((n, own, 128), f32),
        ] + [dma(shape) for shape in sems],
        compiler_params=pltpu.CompilerParams(collective_id=0, has_side_effects=True, vmem_limit_bytes=62 << 20),
        cost_estimate=pl.CostEstimate(flops=2 * T * D * N, bytes_accessed=2 * D * (T + N), transcendentals=T * N),
    )(partials, norm_gain[None, :], head_weight.T, next_ids[None, :], lengths)
    return out, target.reshape(own)


def solution(mesh):
    return jax.shard_map(
        on_device,
        mesh=mesh,
        in_specs=(P("tensor", "groups", None), P(), P(None, "tensor"), P("groups"), P("groups")),
        out_specs=(P(("groups", "tensor"), None), P(("groups", "tensor"))),
        check_vma=False,
    )
```
